32 devices in a mesh: grp: 4 (over z), dev: 8 (over y, x, core).
Axes of the slice: x: 2, y: 2, z: 4, core: 2. Of those that a mesh axis runs over, the one named last changes fastest.
Arguments:
- old_fields: float32 [3, 256, 32, 1024], P(None, ('grp', 'dev')), as said below
- old_counts: int32 [32], replicated, may hold values from 2 to 6, as said below
Outputs:
- pressure_out: float32 [128, 256, 128], P('grp', 'dev')
- residual: float32 [128, 256, 128], P('grp', 'dev')
The draws below stay inside these ranges and needn't reach their ends.
Inputs may be any that keep to these rules, and one draw needn't show every extreme that they name: `old_counts`: the counts sum to 128; each device's first box number, start[e], lies between e * 4 and e * 4 + 4 / 2; the slots of a device beyond its count hold data that belongs to no box. `old_fields`: coefficient entries (component 2) are positive; components 0 and 1 are real-valued of order one.
All inputs are finite; a program needn't handle non-finite values.
Results may differ from the reference program's by a relative error of at most 0.0003.
Values sent between devices are 32-bit elements; how exact they have to be, the bound alone decides.
A program may use at most 64 MiB of HBM per device.

```python
import jax
import jax.numpy as jnp
from jax import lax

BOX = 32
BOX_DEV = 4
CAPO = 8
SLOTS = 256
NBOX = 128
NX = 128
NY = 256
NZ = 128
N_GRP = 4
N_DEV = 8


def draw_old_counts(key, part):
    devices = NBOX // BOX_DEV
    half_box = BOX_DEV // 2
    first_key, second_key = jax.random.split(jax.random.fold_in(key, 11))
    shifts = jax.random.randint(first_key, (devices + 1,), 0, half_box + 1)
    chosen = jax.random.randint(second_key, (), 2, devices - 2)
    shifts = shifts.at[chosen].set(half_box).at[1].set(half_box).at[devices - 1].set(half_box)
    shifts = shifts.at[0].set(0).at[devices].set(0)
    return (BOX_DEV + shifts[1:] - shifts[:-1]).astype(jnp.int32)


def draw_old_fields(key, part):
    keys = jax.random.split(jax.random.fold_in(key, 23), 3)
    shape = (SLOTS, BOX, BOX * BOX)
    pressure = jax.random.normal(keys[0], shape, jnp.float32)
    right_side = jax.random.normal(keys[1], shape, jnp.float32)
    coefficient = jnp.exp(jax.random.uniform(keys[2], shape, jnp.float32, -2.3, 2.3))
    return jnp.stack([pressure, right_side, coefficient]).astype(jnp.float32)


def setup_inputs(seed: int = 0) -> dict:
    seeds = jax.random.split(jax.random.key(seed), 3)
    old_fields = draw_old_fields(jax.random.fold_in(seeds[2], 71), 0)
    old_counts = draw_old_counts(jax.random.fold_in(seeds[2], 71), 0)
    return dict(old_fields=old_fields, old_counts=old_counts)


def beta_parts(coefficient):
    padded = jnp.pad(coefficient, 1)
    centre = padded[1:-1, 1:-1, 1:-1]
    sizes = centre.shape
    betas = []
    for axis_id in range(3):
        for offset in (0, 2):
            starts = [1, 1, 1]
            starts[axis_id] = offset
            neighbour = lax.dynamic_slice(padded, starts, sizes)
            betas.append((0.5 * (centre + neighbour), axis_id, offset))
    return betas


def beta_phi(pressure, betas):
    padded = jnp.pad(pressure, 1)
    sizes = pressure.shape
    total = jnp.zeros(sizes, jnp.float32)
    for beta, axis_id, offset in betas:
        starts = [1, 1, 1]
        starts[axis_id] = offset
        total = total + beta * lax.dynamic_slice(padded, starts, sizes)
    return total


def reference(old_fields, old_counts):
    ends = jnp.cumsum(old_counts).astype(jnp.int32)
    starts = (ends - old_counts).astype(jnp.int32)
    wanted = jnp.arange(NBOX, dtype=jnp.int32)
    owner_dev = jnp.sum((ends[None, :] <= wanted[:, None]).astype(jnp.int32), axis=1).astype(jnp.int32)
    slot_id = (owner_dev * CAPO + wanted - starts[owner_dev]).astype(jnp.int32)
    moved = jnp.take(old_fields, slot_id, axis=1)
    moved = moved.reshape(3, N_GRP, N_DEV, BOX_DEV, BOX, BOX, BOX)
    moved = jnp.transpose(moved, (0, 1, 4, 2, 5, 3, 6)).reshape(3, NX, NY, NZ)
    pressure = moved[0]
    right_side = moved[1]
    coefficient = moved[2]
    betas = beta_parts(coefficient)
    beta_sum = betas[0][0]
    for beta, axis_id, offset in betas[1:]:
        beta_sum = beta_sum + beta
    parity = (lax.broadcasted_iota(jnp.int32, (NX, NY, NZ), 0) + lax.broadcasted_iota(jnp.int32, (NX, NY, NZ), 1) + lax.broadcasted_iota(jnp.int32, (NX, NY, NZ), 2)) % 2
    red_mask = parity == 0
    first = jnp.where(red_mask, (right_side + beta_phi(pressure, betas)) / beta_sum, pressure)
    second = jnp.where(red_mask, first, (right_side + beta_phi(first, betas)) / beta_sum)
    residual = right_side - (beta_sum * second - beta_phi(second, betas))
    return second, residual
```

```python
import functools

import jax
import jax.numpy as jnp
from jax import lax
from jax.experimental import pallas as pl
from jax.experimental.pallas import tpu as pltpu
from jax.sharding import PartitionSpec as P

MESH = pl.DeviceIdType.MESH
LANES = 128
TOP = 8


def kernel(n_grp, n_dev, counts, fields, out_p, out_r,
           own_b, own_p, own_f, snd_b, snd_p, snd_f, got_b, got_p, got_f,
           pa, pb, pc, h, f, s, rinv, sx, gx, sh0, sh1, gh0, gh1,
           in_sem, snd_sem, got_sem, hs_sem, hg_sem):
    edge = h.shape[1] - 2 * TOP
    sh, gh = (sh0, sh1), (gh0, gh1)
    grp, dev = lax.axis_index("grp"), lax.axis_index("dev")
    me = grp * n_dev + dev
    last = n_grp * n_dev - 1
    mine = (own_b, own_p, own_f)
    comps = (2, 0, 1)
    loads = []
    for i in range(3):
        copy = pltpu.make_async_copy(
            fields.at[comps[i], pl.ds(0, own_b.shape[0])], mine[i], in_sem.at[i])
        copy.start()
        loads.append(copy)

    has = (dev > 0, dev < n_dev - 1, grp > 0, grp < n_grp - 1)
    peer = ((grp, dev - 1), (grp, dev + 1), (grp - 1, dev), (grp + 1, dev))
    has_prev, has_next = me > 0, me < last
    prev_far = jnp.logical_and(has_prev, dev == 0)
    next_far = jnp.logical_and(has_next, dev == n_dev - 1)
    before, after = me - 1, me + 1
    prev_id = (before // n_dev, before % n_dev)
    next_id = (after // n_dev, after % n_dev)

    barrier = pltpu.get_barrier_semaphore()
    total = jnp.int32(0)
    for flag, target in list(zip(has, peer)) + [(prev_far, prev_id), (next_far, next_id)]:
        total = total + flag.astype(jnp.int32)

        @pl.when(flag)
        def _(target=target):
            pl.semaphore_signal(barrier, inc=1, device_id=target, device_id_type=MESH)

    start = lax.fori_loop(0, me, lambda i, acc: acc + counts[i], jnp.int32(0))
    k = jnp.clip(start - me * 4, 0, 2)

    zero_plane = jnp.zeros(h.shape[1:], jnp.float32)

    def clear(y, _):
        for ref in (pa, pb, pc, h):
            ref[y] = zero_plane
        return 0

    lax.fori_loop(0, edge + 2, clear, 0)
    pl.semaphore_wait(barrier, total)

    lane = lax.broadcasted_iota(jnp.int32, (8, 1024), 1)
    row = lax.broadcasted_iota(jnp.int32, (8, 1024), 0)
    black_box = (row + lane + lane // 32) % 2 == 1

    regrid = [
        pltpu.make_async_remote_copy(
            src_ref=src, dst_ref=dst, send_sem=snd_sem.at[i], recv_sem=got_sem.at[i],
            device_id=next_id, device_id_type=MESH)
        for i, (src, dst) in enumerate(((snd_b, got_b), (snd_p, got_p), (snd_f, got_f)))
    ]
    for i in range(3):
        loads[i].wait()
        for t in range(edge // 8):
            tile = slice(8 * t, 8 * t + 8)
            first, second = mine[i][4 - k, tile, :], mine[i][5 - k, tile, :]
            if i == 1:
                snd_p[tile, :] = jnp.where(black_box, first, pltpu.roll(second, 1, 0))
            else:
                dst = (snd_b, None, snd_f)[i]
                dst[0, tile, :] = first
                dst[1, tile, :] = second

        @pl.when(has_next)
        def _(i=i):
            regrid[i].start()

    block = lax.broadcasted_iota(jnp.int32, (edge, LANES), 1) // 32
    in0, in1, in2 = block == 0, block == 1, block == 2

    def pick(parts):
        return jnp.where(in0, parts[0], jnp.where(in1, parts[1], jnp.where(in2, parts[2], parts[3])))

    def boxes_to_rows(i, yh):
        cols = pl.ds(pl.multiple_of(yh * LANES, LANES), LANES)
        ref = mine[i]
        own = [ref[jnp.maximum(c - k, 0), :, cols] for c in range(4)]
        if i == 1:
            low0 = got_p[:, cols]
            low1 = pltpu.roll(low0.reshape(edge // 8, 8, LANES), 7, 1).reshape(edge, LANES)
        else:
            got = (got_b, None, got_f)[i]
            low0, low1 = got[0, :, cols], got[1, :, cols]
        boxes = [jnp.where(k >= 1, low0, own[0]), jnp.where(k >= 2, low1, own[1]), own[2], own[3]]
        turned = [boxes[0]] + [pltpu.roll(boxes[c], 32 * c, 1) for c in range(1, 4)]
        rows = []
        for j in range(4):
            value = pick([turned[(q - j) % 4] for q in range(4)])
            rows.append(value if j == 0 else pltpu.roll(value, LANES - 32 * j, 1))
        return rows

    for i in range(3):

        @pl.when(has_prev)
        def _(i=i):
            regrid[i].wait_recv()

        def place(yh, _, i=i):
            rows = boxes_to_rows(i, yh)
            for j in range(4):
                y = yh * 4 + j
                if i == 2:
                    f[y] = rows[j]
                else:
                    ref, value, at = (h, 0.5 * rows[j], edge) if i == 0 else (pa, rows[j], 0)
                    ref[y + 1, TOP:TOP + edge, :] = value
                    for side in range(2):
                        sx[side + 2, pl.ds(at + y, 1), :] = (
                            value[0:1] if side == 0 else value[edge - 1:edge])
            return 0

        lax.fori_loop(0, edge // 4, place, 0)
        if i == 1:
            for side in range(2):
                y = 1 if side == 0 else edge
                sx[side, 0:edge, :] = pa[y, TOP:TOP + edge, :]
                sx[side, edge:2 * edge, :] = h[y, TOP:TOP + edge, :]

            def halo(src, dst, slot):
                return [
                    pltpu.make_async_remote_copy(
                        src_ref=src(w), dst_ref=dst(w ^ 1),
                        send_sem=hs_sem.at[slot, w], recv_sem=hg_sem.at[slot, w ^ 1],
                        device_id=peer[w], device_id_type=MESH)
                    for w in range(4)
                ]

            def arrivals(src, dst, slot):
                return [
                    pltpu.make_async_remote_copy(
                        src_ref=src(w), dst_ref=dst(w),
                        send_sem=hs_sem.at[slot, w], recv_sem=hg_sem.at[slot, w],
                        device_id=peer[w], device_id_type=MESH)
                    for w in range(4)
                ]

            def send(src, dst, slot):
                for w, copy in enumerate(halo(src, dst, slot)):
                    pl.when(has[w])(copy.start)

            def receive(src, dst, slot):
                for w, copy in enumerate(arrivals(src, dst, slot)):
                    pl.when(has[w])(copy.wait_recv)

            def finish(src, dst, slot):
                for w, copy in enumerate(halo(src, dst, slot)):
                    pl.when(has[w])(copy.wait_send)

            wide = (lambda w: sx.at[w], lambda w: gx.at[w])
            send(*wide, 0)

    def unpack(src, targets):
        for side in range(2):
            y = 0 if side == 0 else edge + 1

            @pl.when(has[side])
            def _(side=side, y=y):
                for ref, at in targets:
                    ref[y, TOP:TOP + edge, :] = src(side)[at:at + edge, :]

        for side in range(2):
            x = TOP - 1 if side == 0 else TOP + edge

            @pl.when(has[side + 2])
            def _(side=side, x=x):
                def one(y, _):
                    for ref, at in targets:
                        ref[y + 1, x:x + 1, :] = src(side + 2)[pl.ds(at + y, 1), :]
                    return 0

                lax.fori_loop(0, edge, one, 0, unroll=8)

    lanes = lax.broadcasted_iota(jnp.int32, (edge, LANES), 1)
    xs = lax.broadcasted_iota(jnp.int32, (edge, LANES), 0)
    even = (lanes + xs) % 2 == 0
    low_edge, high_edge = lanes == 0, lanes == LANES - 1

    def near(ref, y):
        centre = ref[y + 1, TOP:TOP + edge, :]
        return centre, [
            ref[y + 1, TOP - 1:TOP - 1 + edge, :],
            ref[y + 1, TOP + 1:TOP + 1 + edge, :],
            ref[y, TOP:TOP + edge, :],
            ref[y + 2, TOP:TOP + edge, :],
            jnp.where(low_edge, 0.0, pltpu.roll(centre, 1, 1)),
            jnp.where(high_edge, 0.0, pltpu.roll(centre, LANES - 1, 1)),
        ]

    def sums(ref, y, with_s):
        p0, p_near = near(ref, y)
        h0, h_near = near(h, y)
        flow, weight = None, None
        for p_n, h_n in zip(p_near, h_near):
            beta = h0 + h_n
            flow = beta * p_n if flow is None else flow + beta * p_n
            if with_s:
                weight = beta if weight is None else weight + beta
        return p0, flow, weight

    def pass_over(body):
        def step(i, _):
            for j in range(2):
                body(i * 2 + j, even if j == 0 else jnp.logical_not(even))
            return 0

        lax.fori_loop(0, edge // 2, step, 0)

    def keep(ref, slot, y, value):
        ref[y + 1, TOP:TOP + edge, :] = value
        sh[slot][2, pl.ds(y, 1), :] = value[0:1]
        sh[slot][3, pl.ds(y, 1), :] = value[edge - 1:edge]

    receive(*wide, 0)
    unpack(lambda w: gx.at[w], ((pa, 0), (h, edge)))

    def red(y, mask):
        p0, flow, weight = sums(pa, y, True)
        inverse = 1.0 / weight
        s[y] = weight
        rinv[y] = inverse
        keep(pb, 0, y, jnp.where(mask, (f[y] + flow) * inverse, p0))

    def black(y, mask):
        p0, flow, _ = sums(pb, y, False)
        value = jnp.where(mask, p0, (f[y] + flow) * rinv[y])
        keep(pc, 1, y, value)
        out_p[pl.ds(y, edge, stride=edge), :] = value

    def rest(y, mask):
        p0, flow, _ = sums(pc, y, False)
        out_r[pl.ds(y, edge, stride=edge), :] = f[y] - (s[y] * p0 - flow)

    def exchange(ref, slot):
        for side in range(2):
            y = 1 if side == 0 else edge
            sh[slot][side] = ref[y, TOP:TOP + edge, :]
        ends = (lambda w: sh[slot].at[w], lambda w: gh[slot].at[w])
        send(*ends, slot + 1)
        receive(*ends, slot + 1)
        unpack(lambda w: gh[slot].at[w], ((ref, 0),))

    pass_over(red)
    exchange(pb, 0)
    pass_over(black)
    exchange(pc, 1)
    pass_over(rest)

    for i in range(3):
        @pl.when(has_next)
        def _(i=i):
            regrid[i].wait_send()
    finish(*wide, 0)
    for slot in range(2):
        finish(lambda w: sh[slot].at[w], lambda w: gh[slot].at[w], slot + 1)


def per_device(n_grp, n_dev, old_fields, old_counts):
    slots, edge, width = old_fields.shape[1:]
    held = slots * 3 // 4
    vmem = lambda *shape: pltpu.VMEM(shape, jnp.float32)
    padded = vmem(edge + 2, edge + 2 * TOP, LANES)
    block = vmem(edge, edge, LANES)
    out = jax.ShapeDtypeStruct((edge * edge, LANES), jnp.float32)
    pressure, residual = pl.pallas_call(
        functools.partial(kernel, n_grp, n_dev),
        out_shape=(out, out),
        in_specs=[pl.BlockSpec(memory_space=pltpu.SMEM), pl.BlockSpec(memory_space=pl.ANY)],
        out_specs=[pl.BlockSpec(memory_space=pltpu.VMEM)] * 2,
        scratch_shapes=[vmem(held, edge, width)] * 3
        + [vmem(2, edge, width), vmem(edge, width), vmem(2, edge, width)] * 2
        + [padded] * 4 + [block] * 3
        + [vmem(4, 2 * edge, LANES)] * 2 + [vmem(4, edge, LANES)] * 4
        + [pltpu.SemaphoreType.DMA((3,))] * 3 + [pltpu.SemaphoreType.DMA((3, 4))] * 2,
        compiler_params=pltpu.CompilerParams(
            collective_id=0, has_side_effects=True, vmem_limit_bytes=40 * 1024 * 1024),
        cost_estimate=pl.CostEstimate(
            flops=edge * edge * LANES * 80, bytes_accessed=4 * 1024 * 1024, transcendentals=0),
    )(old_counts, old_fields)
    shape = (edge, edge, LANES)
    return pressure.reshape(shape), residual.reshape(shape)


def solution(mesh):
    placed = (P(None, ("grp", "dev"), None, None), P())
    return jax.shard_map(
        functools.partial(per_device, mesh.shape["grp"], mesh.shape["dev"]),
        mesh=mesh,
        in_specs=placed,
        out_specs=(P("grp", "dev", None), P("grp", "dev", None)),
        check_vma=False,
    )
```

```python
import functools

import jax
import jax.numpy as jnp
from jax import lax
from jax.experimental import pallas as pl
from jax.experimental.pallas import tpu as pltpu
from jax.sharding import PartitionSpec as P

MESH = pl.DeviceIdType.MESH
LANES = 128
TOP = 8
UNROLL = 16


def even_cells(edge):
    lanes = lax.broadcasted_iota(jnp.int32, (edge, LANES), 1)
    xs = lax.broadcasted_iota(jnp.int32, (edge, LANES), 0)
    return (lanes + xs) % 2 == 0


def near(ref, y):
    edge = ref.shape[0] - 2
    lanes = lax.broadcasted_iota(jnp.int32, (edge, LANES), 1)
    centre = ref[y + 1, TOP:TOP + edge, :]
    return centre, [
        ref[y + 1, TOP - 1:TOP - 1 + edge, :],
        ref[y + 1, TOP + 1:TOP + 1 + edge, :],
        ref[y, TOP:TOP + edge, :],
        ref[y + 2, TOP:TOP + edge, :],
        jnp.where(lanes == 0, 0.0, pltpu.roll(centre, 1, 1)),
        jnp.where(lanes == LANES - 1, 0.0, pltpu.roll(centre, LANES - 1, 1)),
    ]


def sums(ref, h, y, with_s):
    p0, p_near = near(ref, y)
    h0, h_near = near(h, y)
    flow, weight = None, None
    for p_n, h_n in zip(p_near, h_near):
        beta = h0 + h_n
        flow = beta * p_n if flow is None else flow + beta * p_n
        if with_s:
            weight = beta if weight is None else weight + beta
    return p0, flow, weight


def pass_over(edge, body):
    even = even_cells(edge)

    def step(i, _):
        for j in range(UNROLL):
            body(i * UNROLL + j, even if j % 2 == 0 else jnp.logical_not(even))
        return 0

    lax.fori_loop(0, edge // UNROLL, step, 0)


def finish_kernel(pressure, pc, h, f, s, out_p, out_r, stage, sem):
    edge = f.shape[0]
    first = pltpu.make_async_copy(pressure, out_p, sem.at[0])
    first.start()

    def rest(y, mask):
        p0, flow, _ = sums(pc, h, y, False)
        stage[pl.ds(y, edge, stride=edge), :] = f[y] - (s[y] * p0 - flow)

    pass_over(edge, rest)
    second = pltpu.make_async_copy(stage, out_r, sem.at[1])
    second.start()
    first.wait()
    second.wait()


def kernel(n_grp, n_dev, counts, fields, out_p, pc, h, f, s,
           own_b, own_p, own_f, snd_b, snd_p, snd_f, got_b, got_p, got_f,
           pa, pb, rinv, sx, gx, sh0, sh1, gh0, gh1,
           in_sem, snd_sem, got_sem, hs_sem, hg_sem):
    edge = h.shape[1] - 2 * TOP
    sh, gh = (sh0, sh1), (gh0, gh1)
    grp, dev = lax.axis_index("grp"), lax.axis_index("dev")
    me = grp * n_dev + dev
    last = n_grp * n_dev - 1
    mine = (own_b, own_p, own_f)
    comps = (2, 0, 1)
    loads = []
    for i in range(3):
        copy = pltpu.make_async_copy(
            fields.at[comps[i], pl.ds(0, own_b.shape[0])], mine[i], in_sem.at[i])
        copy.start()
        loads.append(copy)

    has = (dev > 0, dev < n_dev - 1, grp > 0, grp < n_grp - 1)
    peer = ((grp, dev - 1), (grp, dev + 1), (grp - 1, dev), (grp + 1, dev))
    has_prev, has_next = me > 0, me < last
    prev_far = jnp.logical_and(has_prev, dev == 0)
    next_far = jnp.logical_and(has_next, dev == n_dev - 1)
    before, after = me - 1, me + 1
    prev_id = (before // n_dev, before % n_dev)
    next_id = (after // n_dev, after % n_dev)

    barrier = pltpu.get_barrier_semaphore()
    total = jnp.int32(0)
    for flag, target in list(zip(has, peer)) + [(prev_far, prev_id), (next_far, next_id)]:
        total = total + flag.astype(jnp.int32)

        @pl.when(flag)
        def _(target=target):
            pl.semaphore_signal(barrier, inc=1, device_id=target, device_id_type=MESH)

    start = lax.fori_loop(0, me, lambda i, acc: acc + counts[i], jnp.int32(0))
    k = jnp.clip(start - me * 4, 0, 2)

    zero_plane = jnp.zeros(h.shape[1:], jnp.float32)

    def clear(y, _):
        for ref in (pa, pb, pc, h):
            ref[y] = zero_plane
        return 0

    lax.fori_loop(0, edge + 2, clear, 0)
    pl.semaphore_wait(barrier, total)

    lane = lax.broadcasted_iota(jnp.int32, (8, 1024), 1)
    row = lax.broadcasted_iota(jnp.int32, (8, 1024), 0)
    black_box = (row + lane + lane // 32) % 2 == 1

    regrid = [
        pltpu.make_async_remote_copy(
            src_ref=src, dst_ref=dst, send_sem=snd_sem.at[i], recv_sem=got_sem.at[i],
            device_id=next_id, device_id_type=MESH)
        for i, (src, dst) in enumerate(((snd_b, got_b), (snd_p, got_p), (snd_f, got_f)))
    ]
    for i in range(3):
        loads[i].wait()
        for t in range(edge // 8):
            tile = slice(8 * t, 8 * t + 8)
            first, second = mine[i][4 - k, tile, :], mine[i][5 - k, tile, :]
            if i == 1:
                snd_p[tile, :] = jnp.where(black_box, first, pltpu.roll(second, 1, 0))
            else:
                dst = (snd_b, None, snd_f)[i]
                dst[0, tile, :] = first
                dst[1, tile, :] = second

        @pl.when(has_next)
        def _(i=i):
            regrid[i].start()

    block = lax.broadcasted_iota(jnp.int32, (edge, LANES), 1) // 32
    in0, in1, in2 = block == 0, block == 1, block == 2

    def pick(parts):
        return jnp.where(in0, parts[0], jnp.where(in1, parts[1], jnp.where(in2, parts[2], parts[3])))

    def boxes_to_rows(i, yh):
        cols = pl.ds(pl.multiple_of(yh * LANES, LANES), LANES)
        ref = mine[i]
        own = [ref[jnp.maximum(c - k, 0), :, cols] for c in range(4)]
        if i == 1:
            low0 = got_p[:, cols]
            low1 = pltpu.roll(low0.reshape(edge // 8, 8, LANES), 7, 1).reshape(edge, LANES)
        else:
            got = (got_b, None, got_f)[i]
            low0, low1 = got[0, :, cols], got[1, :, cols]
        boxes = [jnp.where(k >= 1, low0, own[0]), jnp.where(k >= 2, low1, own[1]), own[2], own[3]]
        turned = [boxes[0]] + [pltpu.roll(boxes[c], 32 * c, 1) for c in range(1, 4)]
        rows = []
        for j in range(4):
            value = pick([turned[(q - j) % 4] for q in range(4)])
            rows.append(value if j == 0 else pltpu.roll(value, LANES - 32 * j, 1))
        return rows

    for i in range(3):

        @pl.when(has_prev)
        def _(i=i):
            regrid[i].wait_recv()

        def place(yh, _, i=i):
            rows = boxes_to_rows(i, yh)
            for j in range(4):
                y = yh * 4 + j
                if i == 2:
                    f[y] = rows[j]
                else:
                    ref, value, at = (h, 0.5 * rows[j], edge) if i == 0 else (pa, rows[j], 0)
                    ref[y + 1, TOP:TOP + edge, :] = value
                    for side in range(2):
                        sx[side + 2, pl.ds(at + y, 1), :] = (
                            value[0:1] if side == 0 else value[edge - 1:edge])
            return 0

        lax.fori_loop(0, edge // 4, place, 0)
        if i == 1:
            for side in range(2):
                y = 1 if side == 0 else edge
                sx[side, 0:edge, :] = pa[y, TOP:TOP + edge, :]
                sx[side, edge:2 * edge, :] = h[y, TOP:TOP + edge, :]

            def halo(src, dst, slot):
                return [
                    pltpu.make_async_remote_copy(
                        src_ref=src(w), dst_ref=dst(w ^ 1),
                        send_sem=hs_sem.at[slot, w], recv_sem=hg_sem.at[slot, w ^ 1],
                        device_id=peer[w], device_id_type=MESH)
                    for w in range(4)
                ]

            def arrivals(src, dst, slot):
                return [
                    pltpu.make_async_remote_copy(
                        src_ref=src(w), dst_ref=dst(w),
                        send_sem=hs_sem.at[slot, w], recv_sem=hg_sem.at[slot, w],
                        device_id=peer[w], device_id_type=MESH)
                    for w in range(4)
                ]

            def send(src, dst, slot):
                for w, copy in enumerate(halo(src, dst, slot)):
                    pl.when(has[w])(copy.start)

            def receive(src, dst, slot):
                for w, copy in enumerate(arrivals(src, dst, slot)):
                    pl.when(has[w])(copy.wait_recv)

            def finish(src, dst, slot):
                for w, copy in enumerate(halo(src, dst, slot)):
                    pl.when(has[w])(copy.wait_send)

            wide = (lambda w: sx.at[w], lambda w: gx.at[w])
            send(*wide, 0)

    def unpack(src, targets):
        for side in range(2):
            y = 0 if side == 0 else edge + 1

            @pl.when(has[side])
            def _(side=side, y=y):
                for ref, at in targets:
                    ref[y, TOP:TOP + edge, :] = src(side)[at:at + edge, :]

        for side in range(2):
            x = TOP - 1 if side == 0 else TOP + edge

            @pl.when(has[side + 2])
            def _(side=side, x=x):
                def one(y, _):
                    for ref, at in targets:
                        ref[y + 1, x:x + 1, :] = src(side + 2)[pl.ds(at + y, 1), :]
                    return 0

                lax.fori_loop(0, edge, one, 0, unroll=8)

    def keep(ref, slot, y, value):
        ref[y + 1, TOP:TOP + edge, :] = value
        sh[slot][2, pl.ds(y, 1), :] = value[0:1]
        sh[slot][3, pl.ds(y, 1), :] = value[edge - 1:edge]

    receive(*wide, 0)
    unpack(lambda w: gx.at[w], ((pa, 0), (h, edge)))

    def red(y, mask):
        p0, flow, weight = sums(pa, h, y, True)
        inverse = 1.0 / weight
        s[y] = weight
        rinv[y] = inverse
        keep(pb, 0, y, jnp.where(mask, (f[y] + flow) * inverse, p0))

    def black(y, mask):
        p0, flow, _ = sums(pb, h, y, False)
        value = jnp.where(mask, p0, (f[y] + flow) * rinv[y])
        keep(pc, 1, y, value)
        out_p[pl.ds(y, edge, stride=edge), :] = value

    def exchange(ref, slot):
        for side in range(2):
            y = 1 if side == 0 else edge
            sh[slot][side] = ref[y, TOP:TOP + edge, :]
        ends = (lambda w: sh[slot].at[w], lambda w: gh[slot].at[w])
        send(*ends, slot + 1)
        receive(*ends, slot + 1)
        unpack(lambda w: gh[slot].at[w], ((ref, 0),))

    pass_over(edge, red)
    exchange(pb, 0)
    pass_over(edge, black)
    exchange(pc, 1)

    for i in range(3):
        @pl.when(has_next)
        def _(i=i):
            regrid[i].wait_send()
    finish(*wide, 0)
    for slot in range(2):
        finish(lambda w: sh[slot].at[w], lambda w: gh[slot].at[w], slot + 1)


def per_device(n_grp, n_dev, old_fields, old_counts):
    slots, edge, width = old_fields.shape[1:]
    held = slots * 3 // 4
    vmem = lambda *shape: pltpu.VMEM(shape, jnp.float32)
    array = lambda *shape: jax.ShapeDtypeStruct(shape, jnp.float32)
    near_shape, block = (edge + 2, edge + 2 * TOP, LANES), (edge, edge, LANES)
    out = array(edge * edge, LANES)
    in_vmem = pl.BlockSpec(memory_space=pltpu.VMEM)
    state = pl.pallas_call(
        functools.partial(kernel, n_grp, n_dev),
        out_shape=(out, array(*near_shape), array(*near_shape), array(*block), array(*block)),
        in_specs=[pl.BlockSpec(memory_space=pltpu.SMEM), pl.BlockSpec(memory_space=pltpu.HBM)],
        out_specs=[in_vmem] * 5,
        scratch_shapes=[vmem(held, edge, width)] * 3
        + [vmem(2, edge, width), vmem(edge, width), vmem(2, edge, width)] * 2
        + [vmem(*near_shape)] * 2 + [vmem(*block)]
        + [vmem(4, 2 * edge, LANES)] * 2 + [vmem(4, edge, LANES)] * 4
        + [pltpu.SemaphoreType.DMA((3,))] * 3 + [pltpu.SemaphoreType.DMA((3, 4))] * 2,
        compiler_params=pltpu.CompilerParams(
            collective_id=0, has_side_effects=True, vmem_limit_bytes=49 * 1024 * 1024),
        cost_estimate=pl.CostEstimate(
            flops=edge * edge * LANES * 80, bytes_accessed=4 * 1024 * 1024, transcendentals=0),
    )(old_counts, old_fields)
    in_hbm = pl.BlockSpec(memory_space=pltpu.HBM)
    pressure, residual = pl.pallas_call(
        finish_kernel,
        out_shape=(out, out),
        in_specs=[in_vmem] * 5,
        out_specs=[in_hbm] * 2,
        scratch_shapes=[vmem(edge * edge, LANES), pltpu.SemaphoreType.DMA((2,))],
        compiler_params=pltpu.CompilerParams(vmem_limit_bytes=16 * 1024 * 1024),
        cost_estimate=pl.CostEstimate(
            flops=edge * edge * LANES * 20, bytes_accessed=4 * 1024 * 1024, transcendentals=0),
    )(*state)
    return pressure.reshape(block), residual.reshape(block)


def solution(mesh):
    placed = (P(None, ("grp", "dev"), None, None), P())
    return jax.shard_map(
        functools.partial(per_device, mesh.shape["grp"], mesh.shape["dev"]),
        mesh=mesh,
        in_specs=placed,
        out_specs=(P("grp", "dev", None), P("grp", "dev", None)),
        check_vma=False,
    )
```

```python
import functools

import jax
import jax.numpy as jnp
from jax import lax
from jax.experimental import pallas as pl
from jax.experimental.pallas import tpu as pltpu
from jax.sharding import PartitionSpec as P

MESH = pl.DeviceIdType.MESH
LANES = 128
TOP = 8
UNROLL = 16


def even_cells(edge):
    lanes = lax.broadcasted_iota(jnp.int32, (edge, LANES), 1)
    xs = lax.broadcasted_iota(jnp.int32, (edge, LANES), 0)
    return (lanes + xs) % 2 == 0


def near(ref, y):
    edge = ref.shape[0] - 2
    lanes = lax.broadcasted_iota(jnp.int32, (edge, LANES), 1)
    centre = ref[y + 1, TOP:TOP + edge, :]
    return centre, [
        ref[y + 1, TOP - 1:TOP - 1 + edge, :],
        ref[y + 1, TOP + 1:TOP + 1 + edge, :],
        ref[y, TOP:TOP + edge, :],
        ref[y + 2, TOP:TOP + edge, :],
        jnp.where(lanes == 0, 0.0, pltpu.roll(centre, 1, 1)),
        jnp.where(lanes == LANES - 1, 0.0, pltpu.roll(centre, LANES - 1, 1)),
    ]


def rows_of(ref):
    return ref.reshape(ref.shape[0] * ref.shape[1], LANES)


def across(ref, x, y=0):
    pitch, edge = ref.shape[1], ref.shape[0] - 2
    return pl.ds((y + 1) * pitch + TOP + x, edge, stride=pitch)


def near_x(ref, x):
    edge = ref.shape[0] - 2
    lanes = lax.broadcasted_iota(jnp.int32, (edge, LANES), 1)
    rows = rows_of(ref)
    centre = rows[across(ref, x), :]
    return centre, [
        rows[across(ref, x - 1), :],
        rows[across(ref, x + 1), :],
        rows[across(ref, x, -1), :],
        rows[across(ref, x, 1), :],
        jnp.where(lanes == 0, 0.0, pltpu.roll(centre, 1, 1)),
        jnp.where(lanes == LANES - 1, 0.0, pltpu.roll(centre, LANES - 1, 1)),
    ]


def sums(ref, h, y, with_s, nearby=near):
    p0, p_near = nearby(ref, y)
    h0, h_near = nearby(h, y)
    flow, weight = None, None
    for p_n, h_n in zip(p_near, h_near):
        beta = h0 + h_n
        flow = beta * p_n if flow is None else flow + beta * p_n
        if with_s:
            weight = beta if weight is None else weight + beta
    return p0, flow, weight


def pass_over(edge, body):
    even = even_cells(edge)

    def step(i, _):
        for j in range(UNROLL):
            body(i * UNROLL + j, even if j % 2 == 0 else jnp.logical_not(even))
        return 0

    lax.fori_loop(0, edge // UNROLL, step, 0)


def finish_kernel(pressure, pc, h, f, s, out_p, out_r, stage, sem):
    edge = f.shape[0]
    first = pltpu.make_async_copy(pressure, out_p, sem.at[0])
    first.start()

    def rest(y, mask):
        p0, flow, _ = sums(pc, h, y, False)
        stage[pl.ds(y, edge, stride=edge), :] = f[y] - (s[y] * p0 - flow)

    pass_over(edge, rest)
    second = pltpu.make_async_copy(stage, out_r, sem.at[1])
    second.start()
    first.wait()
    second.wait()


def kernel(n_grp, n_dev, counts, fields, out_p, pc, h, f, s,
           own_b, own_p, own_f, snd_b, snd_p, snd_f, got_b, got_p, got_f,
           pa, pb, rinv, sx, gx, sh0, sh1, gh0, gh1,
           in_sem, snd_sem, got_sem, hs_sem, hg_sem):
    edge = h.shape[1] - 2 * TOP
    sh, gh = (sh0, sh1), (gh0, gh1)
    grp, dev = lax.axis_index("grp"), lax.axis_index("dev")
    me = grp * n_dev + dev
    last = n_grp * n_dev - 1
    mine = (own_b, own_p, own_f)
    comps = (2, 0, 1)
    loads = []
    for i in range(3):
        copy = pltpu.make_async_copy(
            fields.at[comps[i], pl.ds(0, own_b.shape[0])], mine[i], in_sem.at[i])
        copy.start()
        loads.append(copy)

    has = (dev > 0, dev < n_dev - 1, grp > 0, grp < n_grp - 1)
    peer = ((grp, dev - 1), (grp, dev + 1), (grp - 1, dev), (grp + 1, dev))
    has_prev, has_next = me > 0, me < last
    prev_far = jnp.logical_and(has_prev, dev == 0)
    next_far = jnp.logical_and(has_next, dev == n_dev - 1)
    before, after = me - 1, me + 1
    prev_id = (before // n_dev, before % n_dev)
    next_id = (after // n_dev, after % n_dev)

    barrier = pltpu.get_barrier_semaphore()
    total = jnp.int32(0)
    for flag, target in list(zip(has, peer)) + [(prev_far, prev_id), (next_far, next_id)]:
        total = total + flag.astype(jnp.int32)

        @pl.when(flag)
        def _(target=target):
            pl.semaphore_signal(barrier, inc=1, device_id=target, device_id_type=MESH)

    start = lax.fori_loop(0, me, lambda i, acc: acc + counts[i], jnp.int32(0))
    k = jnp.clip(start - me * 4, 0, 2)

    no_face = jnp.zeros((edge, LANES), jnp.float32)
    for ref in (pa, pb, pc, h):
        ref[0, TOP:TOP + edge, :] = no_face
        ref[edge + 1, TOP:TOP + edge, :] = no_face
        rows_of(ref)[across(ref, -1), :] = no_face
        rows_of(ref)[across(ref, edge), :] = no_face

    pl.semaphore_wait(barrier, total)

    lane = lax.broadcasted_iota(jnp.int32, (8, 1024), 1)
    row = lax.broadcasted_iota(jnp.int32, (8, 1024), 0)
    black_box = (row + lane + lane // 32) % 2 == 1

    regrid = [
        pltpu.make_async_remote_copy(
            src_ref=src, dst_ref=dst, send_sem=snd_sem.at[i], recv_sem=got_sem.at[i],
            device_id=next_id, device_id_type=MESH)
        for i, (src, dst) in enumerate(((snd_b, got_b), (snd_p, got_p), (snd_f, got_f)))
    ]
    for i in range(3):
        loads[i].wait()
        for t in range(edge // 8):
            tile = slice(8 * t, 8 * t + 8)
            first, second = mine[i][4 - k, tile, :], mine[i][5 - k, tile, :]
            if i == 1:
                snd_p[tile, :] = jnp.where(black_box, first, pltpu.roll(second, 1, 0))
            else:
                dst = (snd_b, None, snd_f)[i]
                dst[0, tile, :] = first
                dst[1, tile, :] = second

        @pl.when(has_next)
        def _(i=i):
            regrid[i].start()

    block = lax.broadcasted_iota(jnp.int32, (edge, LANES), 1) // 32
    in0, in1, in2 = block == 0, block == 1, block == 2

    def pick(parts):
        return jnp.where(in0, parts[0], jnp.where(in1, parts[1], jnp.where(in2, parts[2], parts[3])))

    def boxes_to_rows(i, yh):
        cols = pl.ds(pl.multiple_of(yh * LANES, LANES), LANES)
        ref = mine[i]
        own = [ref[jnp.maximum(c - k, 0), :, cols] for c in range(4)]
        if i == 1:
            low0 = got_p[:, cols]
            low1 = pltpu.roll(low0.reshape(edge // 8, 8, LANES), 7, 1).reshape(edge, LANES)
        else:
            got = (got_b, None, got_f)[i]
            low0, low1 = got[0, :, cols], got[1, :, cols]
        boxes = [jnp.where(k >= 1, low0, own[0]), jnp.where(k >= 2, low1, own[1]), own[2], own[3]]
        turned = [boxes[0]] + [pltpu.roll(boxes[c], 32 * c, 1) for c in range(1, 4)]
        rows = []
        for j in range(4):
            value = pick([turned[(q - j) % 4] for q in range(4)])
            rows.append(value if j == 0 else pltpu.roll(value, LANES - 32 * j, 1))
        return rows

    for i in range(3):

        @pl.when(has_prev)
        def _(i=i):
            regrid[i].wait_recv()

        def place(yh, _, i=i):
            rows = boxes_to_rows(i, yh)
            for j in range(4):
                y = yh * 4 + j
                if i == 2:
                    f[y] = rows[j]
                else:
                    ref, value = (h, 0.5 * rows[j]) if i == 0 else (pa, rows[j])
                    ref[y + 1, TOP:TOP + edge, :] = value
            return 0

        lax.fori_loop(0, edge // 4, place, 0, unroll=4)
        if i == 1:
            for side in range(2):
                y = 1 if side == 0 else edge
                sx[side, 0:edge, :] = pa[y, TOP:TOP + edge, :]
                sx[side, edge:2 * edge, :] = h[y, TOP:TOP + edge, :]
                x = 0 if side == 0 else edge - 1
                sx[side + 2, 0:edge, :] = rows_of(pa)[across(pa, x), :]
                sx[side + 2, edge:2 * edge, :] = rows_of(h)[across(h, x), :]

            def halo(src, dst, slot):
                return [
                    pltpu.make_async_remote_copy(
                        src_ref=src(w), dst_ref=dst(w ^ 1),
                        send_sem=hs_sem.at[slot, w], recv_sem=hg_sem.at[slot, w ^ 1],
                        device_id=peer[w], device_id_type=MESH)
                    for w in range(4)
                ]

            def arrivals(src, dst, slot):
                return [
                    pltpu.make_async_remote_copy(
                        src_ref=src(w), dst_ref=dst(w),
                        send_sem=hs_sem.at[slot, w], recv_sem=hg_sem.at[slot, w],
                        device_id=peer[w], device_id_type=MESH)
                    for w in range(4)
                ]

            def send(src, dst, slot):
                for w, copy in enumerate(halo(src, dst, slot)):
                    pl.when(has[w])(copy.start)

            def receive(src, dst, slot):
                for w, copy in enumerate(arrivals(src, dst, slot)):
                    pl.when(has[w])(copy.wait_recv)

            def finish(src, dst, slot):
                for w, copy in enumerate(halo(src, dst, slot)):
                    pl.when(has[w])(copy.wait_send)

            wide = (lambda w: sx.at[w], lambda w: gx.at[w])
            send(*wide, 0)

    def unpack(src, targets):
        for side in range(2):
            y = 0 if side == 0 else edge + 1

            @pl.when(has[side])
            def _(side=side, y=y):
                for ref, at in targets:
                    ref[y, TOP:TOP + edge, :] = src(side)[at:at + edge, :]

        for side in range(2):
            x = -1 if side == 0 else edge

            @pl.when(has[side + 2])
            def _(side=side, x=x):
                for ref, at in targets:
                    rows_of(ref)[across(ref, x), :] = src(side + 2)[at:at + edge, :]

    receive(*wide, 0)
    unpack(lambda w: gx.at[w], ((pa, 0), (h, edge)))

    even = even_cells(edge)

    def red(y, mask):
        p0, flow, weight = sums(pa, h, y, True)
        inverse = 1.0 / weight
        s[y] = weight
        rinv[y] = inverse
        pb[y + 1, TOP:TOP + edge, :] = jnp.where(mask, (f[y] + flow) * inverse, p0)

    def black(y, mask):
        p0, flow, _ = sums(pb, h, y, False)
        value = jnp.where(mask, p0, (f[y] + flow) * rinv[y])
        pc[y + 1, TOP:TOP + edge, :] = value
        out_p[pl.ds(y, edge, stride=edge), :] = value

    def send_faces(ref, slot):
        for side in range(2):
            at = 0 if side == 0 else edge - 1
            is_red = even if at % 2 == 0 else jnp.logical_not(even)
            thin = pl.ds(at, edge, stride=edge)
            for w, nearby, rhs, inv in (
                    (side, near, lambda: f[at], lambda: rinv[at]),
                    (side + 2, near_x, lambda: rows_of(f)[thin, :], lambda: rows_of(rinv)[thin, :])):
                p0, flow, weight = sums(ref, h, at, slot == 0, nearby)
                inverse = 1.0 / weight if slot == 0 else inv()
                value = (rhs() + flow) * inverse
                sh[slot][w] = jnp.where(is_red, value, p0) if slot == 0 else jnp.where(is_red, p0, value)
        send(lambda w: sh[slot].at[w], lambda w: gh[slot].at[w], slot + 1)

    def take_faces(ref, slot):
        receive(lambda w: sh[slot].at[w], lambda w: gh[slot].at[w], slot + 1)
        unpack(lambda w: gh[slot].at[w], ((ref, 0),))

    send_faces(pa, 0)
    pass_over(edge, red)
    take_faces(pb, 0)
    send_faces(pb, 1)
    pass_over(edge, black)
    take_faces(pc, 1)

    for i in range(3):
        @pl.when(has_next)
        def _(i=i):
            regrid[i].wait_send()
    finish(*wide, 0)
    for slot in range(2):
        finish(lambda w: sh[slot].at[w], lambda w: gh[slot].at[w], slot + 1)


def per_device(n_grp, n_dev, old_fields, old_counts):
    slots, edge, width = old_fields.shape[1:]
    held = slots * 3 // 4
    vmem = lambda *shape: pltpu.VMEM(shape, jnp.float32)
    array = lambda *shape: jax.ShapeDtypeStruct(shape, jnp.float32)
    near_shape, block = (edge + 2, edge + 2 * TOP, LANES), (edge, edge, LANES)
    out = array(edge * edge, LANES)
    in_vmem = pl.BlockSpec(memory_space=pltpu.VMEM)
    state = pl.pallas_call(
        functools.partial(kernel, n_grp, n_dev),
        out_shape=(out, array(*near_shape), array(*near_shape), array(*block), array(*block)),
        in_specs=[pl.BlockSpec(memory_space=pltpu.SMEM), pl.BlockSpec(memory_space=pltpu.HBM)],
        out_specs=[in_vmem] * 5,
        scratch_shapes=[vmem(held, edge, width)] * 3
        + [vmem(2, edge, width), vmem(edge, width), vmem(2, edge, width)] * 2
        + [vmem(*near_shape)] * 2 + [vmem(*block)]
        + [vmem(4, 2 * edge, LANES)] * 2 + [vmem(4, edge, LANES)] * 4
        + [pltpu.SemaphoreType.DMA((3,))] * 3 + [pltpu.SemaphoreType.DMA((3, 4))] * 2,
        compiler_params=pltpu.CompilerParams(
            collective_id=0, has_side_effects=True, vmem_limit_bytes=49 * 1024 * 1024),
        cost_estimate=pl.CostEstimate(
            flops=edge * edge * LANES * 80, bytes_accessed=4 * 1024 * 1024, transcendentals=0),
    )(old_counts, old_fields)
    in_hbm = pl.BlockSpec(memory_space=pltpu.HBM)
    pressure, residual = pl.pallas_call(
        finish_kernel,
        out_shape=(out, out),
        in_specs=[in_vmem] * 5,
        out_specs=[in_hbm] * 2,
        scratch_shapes=[vmem(edge * edge, LANES), pltpu.SemaphoreType.DMA((2,))],
        compiler_params=pltpu.CompilerParams(vmem_limit_bytes=16 * 1024 * 1024),
        cost_estimate=pl.CostEstimate(
            flops=edge * edge * LANES * 20, bytes_accessed=4 * 1024 * 1024, transcendentals=0),
    )(*state)
    return pressure.reshape(block), residual.reshape(block)


def solution(mesh):
    placed = (P(None, ("grp", "dev"), None, None), P())
    return jax.shard_map(
        functools.partial(per_device, mesh.shape["grp"], mesh.shape["dev"]),
        mesh=mesh,
        in_specs=placed,
        out_specs=(P("grp", "dev", None), P("grp", "dev", None)),
        check_vma=False,
    )
```

```python
import functools

import jax
import jax.numpy as jnp
from jax import lax
from jax.experimental import pallas as pl
from jax.experimental.pallas import tpu as pltpu
from jax.sharding import PartitionSpec as P

MESH = pl.DeviceIdType.MESH
LANES = 128
TOP = 8
UNROLL = 16


def even_cells(edge):
    lanes = lax.broadcasted_iota(jnp.int32, (edge, LANES), 1)
    xs = lax.broadcasted_iota(jnp.int32, (edge, LANES), 0)
    return (lanes + xs) % 2 == 0


def near(ref, y):
    edge = ref.shape[0] - 2
    lanes = lax.broadcasted_iota(jnp.int32, (edge, LANES), 1)
    centre = ref[y + 1, TOP:TOP + edge, :]
    return centre, [
        ref[y + 1, TOP - 1:TOP - 1 + edge, :],
        ref[y + 1, TOP + 1:TOP + 1 + edge, :],
        ref[y, TOP:TOP + edge, :],
        ref[y + 2, TOP:TOP + edge, :],
        jnp.where(lanes == 0, 0.0, pltpu.roll(centre, 1, 1)),
        jnp.where(lanes == LANES - 1, 0.0, pltpu.roll(centre, LANES - 1, 1)),
    ]


def rows_of(ref):
    return ref.reshape(ref.shape[0] * ref.shape[1], LANES)


def across(ref, x, y=0):
    pitch, edge = ref.shape[1], ref.shape[0] - 2
    return pl.ds((y + 1) * pitch + TOP + x, edge, stride=pitch)


def near_x(ref, x):
    edge = ref.shape[0] - 2
    lanes = lax.broadcasted_iota(jnp.int32, (edge, LANES), 1)
    rows = rows_of(ref)
    centre = rows[across(ref, x), :]
    return centre, [
        rows[across(ref, x - 1), :],
        rows[across(ref, x + 1), :],
        rows[across(ref, x, -1), :],
        rows[across(ref, x, 1), :],
        jnp.where(lanes == 0, 0.0, pltpu.roll(centre, 1, 1)),
        jnp.where(lanes == LANES - 1, 0.0, pltpu.roll(centre, LANES - 1, 1)),
    ]


def sums(ref, h, y, with_s, nearby=near):
    p0, p_near = nearby(ref, y)
    h0, h_near = nearby(h, y)
    flow, weight = None, None
    for p_n, h_n in zip(p_near, h_near):
        beta = h0 + h_n
        flow = beta * p_n if flow is None else flow + beta * p_n
        if with_s:
            weight = beta if weight is None else weight + beta
    return p0, flow, weight


def pass_over(edge, body):
    even = even_cells(edge)

    def step(i, _):
        for j in range(UNROLL):
            body(i * UNROLL + j, even if j % 2 == 0 else jnp.logical_not(even))
        return 0

    lax.fori_loop(0, edge // UNROLL, step, 0)


def finish_kernel(pressure, pc, h, f, s, out_p, out_r, stage, sem):
    edge = f.shape[0]
    first = pltpu.make_async_copy(pressure, out_p, sem.at[0])
    first.start()

    def rest(y, mask):
        p0, flow, _ = sums(pc, h, y, False)
        stage[pl.ds(y, edge, stride=edge), :] = f[y] - (s[y] * p0 - flow)

    pass_over(edge, rest)
    second = pltpu.make_async_copy(stage, out_r, sem.at[1])
    second.start()
    first.wait()
    second.wait()


def kernel(n_grp, n_dev, counts, fields, out_p, pc, h, f, s,
           own_b, own_p, own_f, snd_b, snd_p, snd_f, got_b, got_p, got_f,
           pa, pb, rinv, sx, gx, sh0, sh1, gh0, gh1,
           in_sem, snd_sem, got_sem, hs_sem, hg_sem):
    edge = h.shape[1] - 2 * TOP
    sh, gh = (sh0, sh1), (gh0, gh1)
    grp, dev = lax.axis_index("grp"), lax.axis_index("dev")
    me = grp * n_dev + dev
    last = n_grp * n_dev - 1
    mine = (own_b, own_p, own_f)
    comps = (2, 0, 1)
    loads = []
    for i in range(3):
        copy = pltpu.make_async_copy(
            fields.at[comps[i], pl.ds(0, own_b.shape[0])], mine[i], in_sem.at[i])
        copy.start()
        loads.append(copy)

    has = (dev > 0, dev < n_dev - 1, grp > 0, grp < n_grp - 1)
    peer = ((grp, dev - 1), (grp, dev + 1), (grp - 1, dev), (grp + 1, dev))
    has_prev, has_next = me > 0, me < last
    prev_far = jnp.logical_and(has_prev, dev == 0)
    next_far = jnp.logical_and(has_next, dev == n_dev - 1)
    before, after = me - 1, me + 1
    prev_id = (before // n_dev, before % n_dev)
    next_id = (after // n_dev, after % n_dev)

    barrier = pltpu.get_barrier_semaphore()
    total = jnp.int32(0)
    for flag, target in list(zip(has, peer)) + [(prev_far, prev_id), (next_far, next_id)]:
        total = total + flag.astype(jnp.int32)

        @pl.when(flag)
        def _(target=target):
            pl.semaphore_signal(barrier, inc=1, device_id=target, device_id_type=MESH)

    number = lax.broadcasted_iota(jnp.int32, counts.shape, 1)
    start = jnp.sum(jnp.where(number < me, counts[...], 0))
    k = jnp.clip(start - me * 4, 0, 2)

    no_face = jnp.zeros((edge, LANES), jnp.float32)
    for ref in (pa, pb, pc, h):
        ref[0, TOP:TOP + edge, :] = no_face
        ref[edge + 1, TOP:TOP + edge, :] = no_face
        rows_of(ref)[across(ref, -1), :] = no_face
        rows_of(ref)[across(ref, edge), :] = no_face

    pl.semaphore_wait(barrier, total)

    lane = lax.broadcasted_iota(jnp.int32, (8, 1024), 1)
    row = lax.broadcasted_iota(jnp.int32, (8, 1024), 0)
    black_box = (row + lane + lane // 32) % 2 == 1

    regrid = [
        pltpu.make_async_remote_copy(
            src_ref=src, dst_ref=dst, send_sem=snd_sem.at[i], recv_sem=got_sem.at[i],
            device_id=next_id, device_id_type=MESH)
        for i, (src, dst) in enumerate(((snd_b, got_b), (snd_p, got_p), (snd_f, got_f)))
    ]
    for i in range(3):
        loads[i].wait()
        for t in range(edge // 8):
            tile = slice(8 * t, 8 * t + 8)
            first, second = mine[i][4 - k, tile, :], mine[i][5 - k, tile, :]
            if i == 1:
                snd_p[tile, :] = jnp.where(black_box, first, pltpu.roll(second, 1, 0))
            else:
                dst = (snd_b, None, snd_f)[i]
                dst[0, tile, :] = first
                dst[1, tile, :] = second

        @pl.when(has_next)
        def _(i=i):
            regrid[i].start()

    block = lax.broadcasted_iota(jnp.int32, (edge, LANES), 1) // 32
    in0, in1, in2 = block == 0, block == 1, block == 2

    def pick(parts):
        return jnp.where(in0, parts[0], jnp.where(in1, parts[1], jnp.where(in2, parts[2], parts[3])))

    def boxes_to_rows(i, yh):
        cols = pl.ds(pl.multiple_of(yh * LANES, LANES), LANES)
        ref = mine[i]
        own = [ref[jnp.maximum(c - k, 0), :, cols] for c in range(4)]
        if i == 1:
            low0 = got_p[:, cols]
            low1 = pltpu.roll(low0.reshape(edge // 8, 8, LANES), 7, 1).reshape(edge, LANES)
        else:
            got = (got_b, None, got_f)[i]
            low0, low1 = got[0, :, cols], got[1, :, cols]
        boxes = [jnp.where(k >= 1, low0, own[0]), jnp.where(k >= 2, low1, own[1]), own[2], own[3]]
        turned = [boxes[0]] + [pltpu.roll(boxes[c], 32 * c, 1) for c in range(1, 4)]
        rows = []
        for j in range(4):
            value = pick([turned[(q - j) % 4] for q in range(4)])
            rows.append(value if j == 0 else pltpu.roll(value, LANES - 32 * j, 1))
        return rows

    for i in range(3):

        @pl.when(has_prev)
        def _(i=i):
            regrid[i].wait_recv()

        def place(yh, _, i=i):
            rows = boxes_to_rows(i, yh)
            for j in range(4):
                y = yh * 4 + j
                if i == 2:
                    f[y] = rows[j]
                else:
                    ref, value = (h, 0.5 * rows[j]) if i == 0 else (pa, rows[j])
                    ref[y + 1, TOP:TOP + edge, :] = value
            return 0

        lax.fori_loop(0, edge // 4, place, 0, unroll=4)
        if i == 1:
            for side in range(2):
                y = 1 if side == 0 else edge
                sx[side, 0:edge, :] = pa[y, TOP:TOP + edge, :]
                sx[side, edge:2 * edge, :] = h[y, TOP:TOP + edge, :]
                x = 0 if side == 0 else edge - 1
                sx[side + 2, 0:edge, :] = rows_of(pa)[across(pa, x), :]
                sx[side + 2, edge:2 * edge, :] = rows_of(h)[across(h, x), :]

            def halo(src, dst, slot):
                return [
                    pltpu.make_async_remote_copy(
                        src_ref=src(w), dst_ref=dst(w ^ 1),
                        send_sem=hs_sem.at[slot, w], recv_sem=hg_sem.at[slot, w ^ 1],
                        device_id=peer[w], device_id_type=MESH)
                    for w in range(4)
                ]

            def arrivals(src, dst, slot):
                return [
                    pltpu.make_async_remote_copy(
                        src_ref=src(w), dst_ref=dst(w),
                        send_sem=hs_sem.at[slot, w], recv_sem=hg_sem.at[slot, w],
                        device_id=peer[w], device_id_type=MESH)
                    for w in range(4)
                ]

            def send(src, dst, slot):
                for w, copy in enumerate(halo(src, dst, slot)):
                    pl.when(has[w])(copy.start)

            def receive(src, dst, slot):
                for w, copy in enumerate(arrivals(src, dst, slot)):
                    pl.when(has[w])(copy.wait_recv)

            def finish(src, dst, slot):
                for w, copy in enumerate(halo(src, dst, slot)):
                    pl.when(has[w])(copy.wait_send)

            wide = (lambda w: sx.at[w], lambda w: gx.at[w])
            send(*wide, 0)

    def unpack(src, targets):
        for side in range(2):
            y = 0 if side == 0 else edge + 1

            @pl.when(has[side])
            def _(side=side, y=y):
                for ref, at in targets:
                    ref[y, TOP:TOP + edge, :] = src(side)[at:at + edge, :]

        for side in range(2):
            x = -1 if side == 0 else edge

            @pl.when(has[side + 2])
            def _(side=side, x=x):
                for ref, at in targets:
                    rows_of(ref)[across(ref, x), :] = src(side + 2)[at:at + edge, :]

    receive(*wide, 0)
    unpack(lambda w: gx.at[w], ((pa, 0), (h, edge)))

    even = even_cells(edge)

    def red(y, mask):
        p0, flow, weight = sums(pa, h, y, True)
        inverse = 1.0 / weight
        s[y] = weight
        rinv[y] = inverse
        pb[y + 1, TOP:TOP + edge, :] = jnp.where(mask, (f[y] + flow) * inverse, p0)

    def black(y, mask):
        p0, flow, _ = sums(pb, h, y, False)
        value = jnp.where(mask, p0, (f[y] + flow) * rinv[y])
        pc[y + 1, TOP:TOP + edge, :] = value
        out_p[pl.ds(y, edge, stride=edge), :] = value

    def send_faces(ref, slot):
        for side in range(2):
            at = 0 if side == 0 else edge - 1
            is_red = even if at % 2 == 0 else jnp.logical_not(even)
            thin = pl.ds(at, edge, stride=edge)
            for w, nearby, rhs, inv in (
                    (side, near, lambda: f[at], lambda: rinv[at]),
                    (side + 2, near_x, lambda: rows_of(f)[thin, :], lambda: rows_of(rinv)[thin, :])):
                p0, flow, weight = sums(ref, h, at, slot == 0, nearby)
                inverse = 1.0 / weight if slot == 0 else inv()
                value = (rhs() + flow) * inverse
                sh[slot][w] = jnp.where(is_red, value, p0) if slot == 0 else jnp.where(is_red, p0, value)
        send(lambda w: sh[slot].at[w], lambda w: gh[slot].at[w], slot + 1)

    def take_faces(ref, slot):
        receive(lambda w: sh[slot].at[w], lambda w: gh[slot].at[w], slot + 1)
        unpack(lambda w: gh[slot].at[w], ((ref, 0),))

    send_faces(pa, 0)
    pass_over(edge, red)
    take_faces(pb, 0)
    send_faces(pb, 1)
    pass_over(edge, black)
    take_faces(pc, 1)

    for i in range(3):
        @pl.when(has_next)
        def _(i=i):
            regrid[i].wait_send()
    finish(*wide, 0)
    for slot in range(2):
        finish(lambda w: sh[slot].at[w], lambda w: gh[slot].at[w], slot + 1)


def per_device(n_grp, n_dev, old_fields, old_counts):
    slots, edge, width = old_fields.shape[1:]
    held = slots * 3 // 4
    vmem = lambda *shape: pltpu.VMEM(shape, jnp.float32)
    array = lambda *shape: jax.ShapeDtypeStruct(shape, jnp.float32)
    near_shape, block = (edge + 2, edge + 2 * TOP, LANES), (edge, edge, LANES)
    out = array(edge * edge, LANES)
    in_vmem = pl.BlockSpec(memory_space=pltpu.VMEM)
    state = pl.pallas_call(
        functools.partial(kernel, n_grp, n_dev),
        out_shape=(out, array(*near_shape), array(*near_shape), array(*block), array(*block)),
        in_specs=[in_vmem, pl.BlockSpec(memory_space=pltpu.HBM)],
        out_specs=[in_vmem] * 5,
        scratch_shapes=[vmem(held, edge, width)] * 3
        + [vmem(2, edge, width), vmem(edge, width), vmem(2, edge, width)] * 2
        + [vmem(*near_shape)] * 2 + [vmem(*block)]
        + [vmem(4, 2 * edge, LANES)] * 2 + [vmem(4, edge, LANES)] * 4
        + [pltpu.SemaphoreType.DMA((3,))] * 3 + [pltpu.SemaphoreType.DMA((3, 4))] * 2,
        compiler_params=pltpu.CompilerParams(
            collective_id=0, has_side_effects=True, vmem_limit_bytes=49 * 1024 * 1024),
        cost_estimate=pl.CostEstimate(
            flops=edge * edge * LANES * 80, bytes_accessed=4 * 1024 * 1024, transcendentals=0),
    )(old_counts.reshape(1, -1), old_fields)
    in_hbm = pl.BlockSpec(memory_space=pltpu.HBM)
    pressure, residual = pl.pallas_call(
        finish_kernel,
        out_shape=(out, out),
        in_specs=[in_vmem] * 5,
        out_specs=[in_hbm] * 2,
        scratch_shapes=[vmem(edge * edge, LANES), pltpu.SemaphoreType.DMA((2,))],
        compiler_params=pltpu.CompilerParams(vmem_limit_bytes=16 * 1024 * 1024),
        cost_estimate=pl.CostEstimate(
            flops=edge * edge * LANES * 20, bytes_accessed=4 * 1024 * 1024, transcendentals=0),
    )(*state)
    return pressure.reshape(block), residual.reshape(block)


def solution(mesh):
    placed = (P(None, ("grp", "dev"), None, None), P())
    return jax.shard_map(
        functools.partial(per_device, mesh.shape["grp"], mesh.shape["dev"]),
        mesh=mesh,
        in_specs=placed,
        out_specs=(P("grp", "dev", None), P("grp", "dev", None)),
        check_vma=False,
    )
```
